512 devices in a mesh: win: 64 (over x, y, z_hi, core), head: 8 (over z_lo).
Axes of the slice: x: 4, y: 4, z: 16 (z_hi: 2, z_lo: 8; z = z_hi * 8 + z_lo), core: 2. Of those that a mesh axis runs over, the one named last changes fastest.
Arguments:
- query_proj: bfloat16 [8192, 5120], P('win', 'head'), may hold values from -8 to 8
- key_proj: bfloat16 [8192, 5120], P('win', 'head'), may hold values from -8 to 8
- value_proj: bfloat16 [8192, 5120], P('win', 'head'), may hold values from -16 to 16
- latents: bfloat16 [8192, 5120], P('win', 'head'), may hold values from -6 to 6
- out_weight: bfloat16 [5120, 5120], P('win', 'head'), may hold values from -0.078125 to 0.078125
- level_gate: float32 [8, 5120], P(None, 'head'), may hold values from 0.3 to 1.5
- levels: int32 [64], P('win'), may hold values from 0 to 7
- frame_mask: int32 [64, 16], P('win'), may hold values 0 or 1
- seed_block: int32 [1], replicated, may hold values from 0 to 63
Outputs:
- stepped: bfloat16 [8192, 5120], P('win', 'head')
The draws below stay inside these ranges and needn't reach their ends.
All inputs are finite; a program needn't handle non-finite values. No bound on the sum of `frame_mask` on one device may be relied on, other than what follows from the above.
Results may differ from the reference program's by a relative error of at most 0.0065.
Values may be sent and summed in bfloat16 or wider, within the bound.
No kernel may reach another device: no remote copies, remote signals or barrier semaphores. Data moves between devices by JAX's collectives and lax.ppermute only.
A program may use at most 64 MiB of HBM per device.

```python
import jax
import jax.numpy as jnp
from jax import lax

HEADS = 40
HD = 128
D = 5120
TOK = 128
CTX = 16
LEVELS = 8
BLOCKS = 64
TOKENS = 8192


def draw_query_proj(key, part):
    key = jax.random.fold_in(key, 11)
    base = jnp.clip(jax.random.normal(key, (TOKENS, HEADS, HD)), -6.0, 6.0)
    return base.reshape(TOKENS, HEADS * HD).astype(jnp.bfloat16)


def draw_key_proj(key, part):
    key = jax.random.fold_in(key, 23)
    base = jnp.clip(jax.random.normal(key, (TOKENS, HEADS, HD)), -6.0, 6.0)
    return base.reshape(TOKENS, HEADS * HD).astype(jnp.bfloat16)


def set_ends(values, key, smallest, top_value):
    shape = values.shape
    place = [jax.random.randint(jax.random.fold_in(key, axis), (), 0, shape[axis]) for axis in range(len(shape))]
    values = values.at[tuple(place)].set(smallest)
    longest = shape.index(max(shape))
    place[longest] = (place[longest] + 1) % shape[longest]
    return values.at[tuple(place)].set(top_value)


def level_of(own_key, dims, shards, least, largest):
    loudness = 1.0
    for axis_at, blocks in shards:
        heights = jax.random.uniform(jax.random.fold_in(jax.random.fold_in(own_key, 6), axis_at), (blocks,), jnp.float32, least / len(shards), largest / len(shards))
        loudness = loudness * jnp.repeat(jnp.exp(heights), dims[axis_at] // blocks).reshape((-1,) + (1,) * (len(dims) - 1 - axis_at))
    return loudness


def centred(rng, shape, width, bound, shards=(), kind=jnp.bfloat16):
    drawn = jax.random.normal(rng, shape, jnp.float32) * width
    if len(shards) > 0:
        drawn = level_of(rng, shape, shards, -0.22, 0.18) * drawn
    return jnp.clip(drawn, min=-bound, max=bound).astype(kind)


def setup_inputs(seed: int = 0) -> dict:
    key_of = jax.random.split(jax.random.key(seed), 10)
    query_proj = draw_query_proj(jax.random.fold_in(key_of[9], 71), 0)
    key_proj = draw_key_proj(jax.random.fold_in(key_of[9], 71), 0)
    value_proj = centred(key_of[2], (TOKENS, D), 3.0, 16.0, ((0, 64), (1, 8)))
    latents = centred(key_of[3], (TOKENS, D), 1.0, 6.0, ((0, 64), (1, 8)))
    out_weight = centred(key_of[4], (D, D), D ** -0.5, 0.078125, ((0, 64), (1, 8)))
    level_gate = jnp.clip(0.3 + 1.2 * jax.random.uniform(key_of[5], (LEVELS, D), jnp.float32) ** level_of(key_of[5], (LEVELS, D), ((1, 8),), -0.2, 0.2), 0.3, 1.5)
    levels = set_ends(jax.random.randint(key_of[6], (BLOCKS,), 0, LEVELS), jax.random.fold_in(key_of[6], 1), 0, LEVELS - 1).astype(jnp.int32)
    frame_mask = set_ends((jax.random.randint(key_of[7], (BLOCKS, CTX), 0, 4) < 3).astype(jnp.int32), jax.random.fold_in(key_of[7], 1), 0, 1)
    seed_block = jax.random.randint(key_of[8], (1,), 0, BLOCKS).astype(jnp.int32)
    return dict(query_proj=query_proj, key_proj=key_proj, value_proj=value_proj, latents=latents, out_weight=out_weight, level_gate=level_gate, levels=levels, frame_mask=frame_mask, seed_block=seed_block)


def reference(query_proj, key_proj, value_proj, latents, out_weight, level_gate, levels, frame_mask, seed_block):
    score_scale = HD ** -0.5
    query_blocks = query_proj.reshape(BLOCKS, TOK, HEADS, HD)
    key_blocks = key_proj.reshape(BLOCKS, TOK, HEADS, HD)
    value_blocks = value_proj.reshape(BLOCKS, TOK, HEADS, HD)
    lag_list = jnp.arange(CTX + 1, dtype=jnp.int32)

    def one_block(block):
        frame_age = (block - seed_block[0] - 1) % BLOCKS
        source = ((block - lag_list) % BLOCKS).astype(jnp.int32)
        flags = jnp.concatenate([jnp.ones((1,), jnp.int32), frame_mask[block]])
        seen = (lag_list <= frame_age) & (flags == 1)
        query_here = query_blocks[block].astype(jnp.float32)
        key_here = key_blocks[source].astype(jnp.float32)
        value_here = value_blocks[source].astype(jnp.float32)
        scores = jnp.einsum('thd,jshd->htjs', query_here, key_here) * score_scale
        scores = jnp.where(seen[None, None, :, None], scores, -1e30)
        top = jnp.max(scores, axis=(2, 3), keepdims=True)
        expo = jnp.exp(scores - top)
        total = jnp.sum(expo, axis=(2, 3))
        weights = expo.astype(jnp.bfloat16).astype(jnp.float32)
        summed = jnp.einsum('htjs,jshd->thd', weights, value_here)
        return (summed / jnp.transpose(total)[:, :, None]).astype(jnp.bfloat16)

    attended = lax.map(one_block, jnp.arange(BLOCKS, dtype=jnp.int32)).reshape(TOKENS, D)
    projected = jnp.dot(attended, out_weight, preferred_element_type=jnp.float32)
    gate_rows = jnp.repeat(level_gate[levels], TOK, axis=0)
    return (latents.astype(jnp.float32) + gate_rows * projected).astype(jnp.bfloat16)
```

```python
import jax
import jax.numpy as jnp
import numpy as np
from jax import lax
from jax.experimental import pallas as pl
from jax.experimental.pallas import tpu as pltpu
from jax.sharding import Mesh, PartitionSpec as P

HD = 128
TOK = 128
LEVELS = 8
HEADS_HERE = 5
FEAT = 640
HALF = 320
WIDE = 384
HIDDEN = -(2.0**100)
SCORE_SCALE = 1.4426950408889634 * HD**-0.5
AXES = ("x", "y", "zh", "c", "zl")
SIZES = (4, 4, 2, 2, 8)


def move(value, rule):
    pairs = []
    for source, place in enumerate(np.ndindex(*SIZES)):
        target = rule(*place)
        if target is not None:
            pairs.append((source, int(np.ravel_multi_index(target, SIZES))))
    return lax.ppermute(value, AXES, pairs)


def half_of_feature(half, lane):
    return (2 * (lane // 80) + half) * 80 + lane % 80


def selection_tables():
    tables = np.zeros((2, 768, 768), np.float32)
    for mine in range(2):
        for slot, half in enumerate((mine, 1 - mine)):
            base = slot * WIDE
            for lane in range(HALF):
                tables[mine, half_of_feature(half, lane), base + lane] = 1
            for stat in range(24):
                tables[mine, FEAT + stat, base + HALF + stat] = 1
    return tables


def spread_tables():
    tables = np.zeros((2, 2, 128, WIDE), np.float32)
    for half in range(2):
        for lane in range(HALF):
            head = half_of_feature(half, lane) // HD
            tables[half, 0, 64 + head, lane] = 1
            tables[half, 1, 72 + head, lane] = 1
        for head in range(HEADS_HERE):
            tables[half, 0, 64 + head, HALF + 8 + head] = 1
            tables[half, 0, 64 + head, HALF + 16 + head] = 1
    return tables


SELECTION = selection_tables()
SPREAD = spread_tables()


def dot_f32(a, b):
    return jnp.dot(a, b, preferred_element_type=jnp.float32)


def attend_kernel(code_ref, qa_ref, qb_ref, kv0, kv1, kv2, kv3, kv4, select_ref, mine_ref, theirs_ref):
    kvs = (kv0, kv1, kv2, kv3, kv4)
    lane = lax.broadcasted_iota(jnp.int32, (1, 128), 1)
    lanes = lax.broadcasted_iota(jnp.int32, (TOK, 128), 1)
    for r in range(4):
        q_ref = qa_ref if r % 2 == 0 else qb_ref
        zf = r // 2
        flags = q_ref[zf, TOK : TOK + 16, 0:128].astype(jnp.float32)[0:1]
        biases = []
        for d in range(5):
            code = code_ref[r, d]
            hit = jnp.sum(jnp.where(lane == code - 1, flags, 0.0), axis=1, keepdims=True)
            hit = jnp.where(code == 0, 1.0, hit)
            biases.append(jnp.broadcast_to(jnp.where(hit > 0.5, 0.0, HIDDEN), (1, 128)))
        bias = jnp.concatenate(biases, axis=1)
        acc = jnp.zeros((TOK, 2 * WIDE), jnp.float32)
        stats = jnp.zeros((TOK, 128), jnp.float32)
        for h in range(HEADS_HERE):
            cols = slice(h * HD, (h + 1) * HD)
            keys = jnp.concatenate([kv[0, :, cols] for kv in kvs], axis=0)
            values = jnp.concatenate([kv[1, :, cols] for kv in kvs], axis=0)
            scores = lax.dot_general(
                q_ref[zf, 0:TOK, cols], keys, (((1,), (1,)), ((), ())), preferred_element_type=jnp.float32
            )
            scores = scores * SCORE_SCALE + bias
            top = jnp.max(scores, axis=1, keepdims=True).astype(jnp.bfloat16).astype(jnp.float32)
            expo = jnp.exp2(scores - top)
            total = jnp.sum(expo, axis=1, keepdims=True)
            total_hi = total.astype(jnp.bfloat16).astype(jnp.float32)
            summed = dot_f32(expo.astype(jnp.bfloat16), values)
            acc = acc + dot_f32(summed.astype(jnp.bfloat16), select_ref[cols, :])
            stats = jnp.where(lanes == h, top, stats)
            stats = jnp.where(lanes == 8 + h, total_hi, stats)
            stats = jnp.where(lanes == 16 + h, total - total_hi, stats)
        acc = acc + dot_f32(stats.astype(jnp.bfloat16), select_ref[FEAT : FEAT + 128, :])
        mine_ref[r] = acc[:, :WIDE].astype(jnp.bfloat16)
        theirs_ref[r] = acc[:, WIDE:].astype(jnp.bfloat16)


def spread(factor, table):
    high = factor.astype(jnp.bfloat16)
    low = (factor - high.astype(jnp.float32)).astype(jnp.bfloat16)
    return dot_f32(high, table) + dot_f32(low, table)


def merge(first, second, table):
    one, two = first.astype(jnp.float32), second.astype(jnp.float32)
    s1, s2 = one[:, 256:], two[:, 256:]
    top = jnp.maximum(s1, s2)
    joined = one * spread(jnp.exp2(s1 - top), table) + two * spread(jnp.exp2(s2 - top), table)
    return joined, top


def merge_cores_kernel(mine_ref, got_ref, table_ref, keep_ref, send_ref):
    lanes = lax.broadcasted_iota(jnp.int32, (TOK, 128), 1)
    for r in range(4):
        joined, top = merge(mine_ref[r], got_ref[r ^ 1], table_ref[0])
        tail = joined[:, 256:]
        high = tail.astype(jnp.bfloat16).astype(jnp.float32)
        tail = jnp.where(lanes >= 80, tail + pltpu.roll(tail - high, 8, 1), high)
        tail = jnp.where((lanes >= 64) & (lanes < 72), top, tail)
        out_ref = keep_ref if r < 2 else send_ref
        out_ref[r % 2, :, 0:256] = joined[:, :256].astype(jnp.bfloat16)
        out_ref[r % 2, :, 256:384] = tail.astype(jnp.bfloat16)


def merge_last_kernel(keep_ref, got_ref, table_ref, out_ref):
    lanes = lax.broadcasted_iota(jnp.int32, (TOK, 128), 1)
    for r in range(2):
        joined, top = merge(keep_ref[r], got_ref[r], table_ref[0])
        tail = joined[:, 256:]
        total = tail + pltpu.roll(tail, 120, 1)
        used = (lanes >= 72) & (lanes < 72 + HEADS_HERE)
        inverse = jnp.where(used, 1.0 / jnp.where(used, total, 1.0), 0.0)
        done = joined * spread(inverse, table_ref[1])
        out_ref[r] = done[:, :HALF].astype(jnp.bfloat16)


def project_kernel(place_ref, own_ref, *refs):
    lefts, rights = refs[0:7], refs[7:14]
    w_ref, keep_ref, send_ref, acc = refs[14:]
    zl = place_ref[0]
    acc[...] = dot_f32(own_ref[...].reshape(2 * TOK, HALF), w_ref[zl])
    for k in range(1, 8):

        @pl.when(zl - k >= 0)
        def from_left():
            acc[...] += dot_f32(lefts[k - 1][...].reshape(2 * TOK, HALF), w_ref[jnp.maximum(zl - k, 0)])

        @pl.when(zl + k <= 7)
        def from_right():
            acc[...] += dot_f32(rights[k - 1][...].reshape(2 * TOK, HALF), w_ref[jnp.minimum(zl + k, 7)])

    keep_ref[...] = acc[0:TOK]
    send_ref[...] = acc[TOK:].astype(jnp.bfloat16)


VMEM = pl.BlockSpec(memory_space=pltpu.VMEM)
SMEM = pl.BlockSpec(memory_space=pltpu.SMEM)
PARAMS = pltpu.CompilerParams(vmem_limit_bytes=40 * 1024 * 1024)


def bf16(*shape):
    return jax.ShapeDtypeStruct(shape, jnp.bfloat16)


def on_device(query, key, value, latents, out_weight, level_gate, levels, frame_mask, seed_block):
    x, y = lax.axis_index("x"), lax.axis_index("y")
    zh, c, zl = lax.axis_index("zh"), lax.axis_index("c"), lax.axis_index("zl")
    column = 4 * x + y

    weight_half = lax.all_gather(out_weight, ("x", "y", "zh"), axis=0, tiled=True).reshape(8, HALF, FEAT)

    flags = jnp.pad(frame_mask.astype(jnp.bfloat16), ((0, 15), (0, FEAT - 16)))
    q_own = jnp.concatenate([query, flags], axis=0)
    q_far = move(q_own, lambda x, y, h, c, l: (x, y, 1 - h, c, l))
    qa = jnp.stack([q_own, q_far])
    qb = move(qa, lambda x, y, h, c, l: (x, y, h, 1 - c, l))

    kv0 = jnp.stack([key, value])
    kv4 = move(kv0, lambda x, y, h, c, l: ((x + 1) % 4, y, h, c, l))
    kv1 = move(jnp.where(y == 3, kv4, kv0), lambda x, y, h, c, l: (x, (y + 1) % 4, h, c, l))
    kv3 = move(jnp.where(y == 0, kv0, kv4), lambda x, y, h, c, l: (x, (y - 1) % 4, h, c, l))
    kv2 = move(jnp.where(y >= 2, kv4, kv0), lambda x, y, h, c, l: (x, (y + 2) % 4, h, c, l))

    r = jnp.arange(4, dtype=jnp.int32)[:, None]
    d = jnp.arange(5, dtype=jnp.int32)[None, :]
    inner = 2 * (zh ^ (r >> 1)) + (c ^ (r & 1))
    lag = 4 * d + inner - (2 * zh + c)
    age = (4 * column + inner - seed_block[0] - 1) % 64
    code = jnp.where((lag == 0) | ((lag > 0) & (lag <= 16) & (lag <= age)), lag, -1).astype(jnp.int32)

    select = lax.dynamic_index_in_dim(jnp.asarray(SELECTION, jnp.bfloat16), c, keepdims=False)
    table = lax.dynamic_index_in_dim(jnp.asarray(SPREAD, jnp.bfloat16), c, keepdims=False)

    mine, theirs = pl.pallas_call(
        attend_kernel,
        out_shape=(bf16(4, TOK, WIDE), bf16(4, TOK, WIDE)),
        in_specs=[SMEM] + [VMEM] * 8,
        out_specs=(VMEM, VMEM),
        compiler_params=PARAMS,
        name="attend",
    )(code, qa, qb, kv0, kv1, kv2, kv3, kv4, select)
    got = move(theirs, lambda x, y, h, c, l: (x, y, h, 1 - c, l))
    keep, send = pl.pallas_call(
        merge_cores_kernel,
        out_shape=(bf16(2, TOK, WIDE), bf16(2, TOK, WIDE)),
        in_specs=[VMEM] * 3,
        out_specs=(VMEM, VMEM),
        compiler_params=PARAMS,
        name="merge_cores",
    )(mine, got, table)
    got = move(send, lambda x, y, h, c, l: (x, y, 1 - h, c, l))
    attended = pl.pallas_call(
        merge_last_kernel,
        out_shape=bf16(2, TOK, HALF),
        in_specs=[VMEM] * 3,
        out_specs=VMEM,
        compiler_params=PARAMS,
        name="merge_last",
    )(keep, got, table)

    lefts, rights = [], []
    left = right = attended
    for k in range(7):
        left = move(left, lambda x, y, h, c, l: (x, y, h, c, l + 1) if l < 7 else None)
        right = move(right, lambda x, y, h, c, l: (x, y, h, c, l - 1) if l > 0 else None)
        lefts.append(left)
        rights.append(right)

    keep, send = pl.pallas_call(
        project_kernel,
        out_shape=(jax.ShapeDtypeStruct((TOK, FEAT), jnp.float32), bf16(TOK, FEAT)),
        in_specs=[SMEM] + [VMEM] * 16,
        out_specs=(VMEM, VMEM),
        scratch_shapes=[pltpu.VMEM((2 * TOK, FEAT), jnp.float32)],
        compiler_params=PARAMS,
        name="project",
    )(zl.reshape(1), attended, *lefts, *rights, weight_half)
    got = move(send, lambda x, y, h, c, l: (x, y, h, 1 - c, l))

    level_pick = (jnp.arange(LEVELS, dtype=jnp.int32) == levels[0]).astype(jnp.float32)
    gate_row = jnp.sum(level_pick[:, None] * level_gate, axis=0)
    projected = keep + got.astype(jnp.float32)
    return (latents.astype(jnp.float32) + gate_row[None, :] * projected).astype(jnp.bfloat16)


def solution(mesh):
    fine = Mesh(mesh.devices.reshape(SIZES), AXES)
    win = ("x", "y", "zh", "c")
    in_specs = (
        P(win, "zl"),
        P(win, "zl"),
        P(win, "zl"),
        P(win, "zl"),
        P(win, "zl"),
        P(None, "zl"),
        P(win),
        P(win, None),
        P(),
    )
    return jax.shard_map(
        on_device, mesh=fine, in_specs=in_specs, out_specs=P(win, "zl"), check_vma=False
    )
```

```python
import jax
import jax.numpy as jnp
import numpy as np
from jax import lax
from jax.experimental import pallas as pl
from jax.experimental.pallas import tpu as pltpu
from jax.sharding import Mesh, PartitionSpec as P

HD = 128
TOK = 128
LEVELS = 8
HEADS_HERE = 5
FEAT = 640
HALF = 320
WIDE = 384
HIDDEN = -(2.0**100)
SCORE_SCALE = 1.4426950408889634 * HD**-0.5
AXES = ("x", "y", "zh", "c", "zl")
SIZES = (4, 4, 2, 2, 8)


def move(value, rule):
    pairs = []
    for source, place in enumerate(np.ndindex(*SIZES)):
        target = rule(*place)
        if target is not None:
            pairs.append((source, int(np.ravel_multi_index(target, SIZES))))
    return lax.ppermute(value, AXES, pairs)


def half_of_feature(half, lane):
    return (2 * (lane // 80) + half) * 80 + lane % 80


def selection_tables():
    tables = np.zeros((2, 768, 768), np.float32)
    for mine in range(2):
        for slot, half in enumerate((mine, 1 - mine)):
            base = slot * WIDE
            for lane in range(HALF):
                tables[mine, half_of_feature(half, lane), base + lane] = 1
            for stat in range(24):
                tables[mine, FEAT + stat, base + HALF + stat] = 1
    return tables


def spread_tables():
    tables = np.zeros((2, 2, 128, WIDE), np.float32)
    for half in range(2):
        for lane in range(HALF):
            head = half_of_feature(half, lane) // HD
            tables[half, 0, 64 + head, lane] = 1
            tables[half, 1, 72 + head, lane] = 1
        for head in range(HEADS_HERE):
            tables[half, 0, 64 + head, HALF + 8 + head] = 1
            tables[half, 0, 64 + head, HALF + 16 + head] = 1
    return tables


SELECTION = selection_tables()
SPREAD = spread_tables()


def dot_f32(a, b):
    return jnp.dot(a, b, preferred_element_type=jnp.float32)


def attend_kernel(code_ref, qa_ref, qb_ref, kv0, kv1, kv2, kv3, kv4, select_ref, mine_ref, theirs_ref, all_ref):
    kvs = (kv0, kv1, kv2, kv3, kv4)
    lane = lax.broadcasted_iota(jnp.int32, (1, 128), 1)
    lanes = lax.broadcasted_iota(jnp.int32, (TOK, 128), 1)
    biases = []
    for r in range(4):
        q_ref = qa_ref if r % 2 == 0 else qb_ref
        flags = q_ref[r // 2, TOK : TOK + 16, 0:128].astype(jnp.float32)[0:1]
        row = []
        for d in range(5):
            code = code_ref[r, d]
            hit = jnp.sum(jnp.where(lane == code - 1, flags, 0.0), axis=1, keepdims=True)
            hit = jnp.where(code == 0, 1.0, hit)
            row.append(jnp.broadcast_to(jnp.where(hit > 0.5, 0.0, HIDDEN), (1, 128)))
        biases.append(jnp.concatenate(row, axis=1))
    stats = [jnp.zeros((TOK, 128), jnp.float32) for r in range(4)]
    for h in range(HEADS_HERE):
        cols = slice(h * HD, (h + 1) * HD)
        keys = jnp.concatenate([kv[0, :, cols] for kv in kvs], axis=0)
        values = jnp.concatenate([kv[1, :, cols] for kv in kvs], axis=0)
        queries = jnp.concatenate(
            [(qa_ref if r % 2 == 0 else qb_ref)[r // 2, 0:TOK, cols] for r in range(4)], axis=0
        )
        scores = lax.dot_general(queries, keys, (((1,), (1,)), ((), ())), preferred_element_type=jnp.float32)
        parts = []
        for r in range(4):
            part = scores[r * TOK : (r + 1) * TOK] * SCORE_SCALE + biases[r]
            top = jnp.max(part, axis=1, keepdims=True).astype(jnp.bfloat16).astype(jnp.float32)
            expo = jnp.exp2(part - top)
            total = jnp.sum(expo, axis=1, keepdims=True)
            total_hi = total.astype(jnp.bfloat16).astype(jnp.float32)
            parts.append(expo.astype(jnp.bfloat16))
            stats[r] = jnp.where(lanes == h, top, stats[r])
            stats[r] = jnp.where(lanes == 8 + h, total_hi, stats[r])
            stats[r] = jnp.where(lanes == 16 + h, total - total_hi, stats[r])
        summed = dot_f32(jnp.concatenate(parts, axis=0), values)
        all_ref[:, cols] = summed.astype(jnp.bfloat16)
    for r in range(4):
        all_ref[r * TOK : (r + 1) * TOK, FEAT:] = stats[r].astype(jnp.bfloat16)
    mine_ref[...] = dot_f32(all_ref[...], select_ref[:, :WIDE]).astype(jnp.bfloat16).reshape(4, TOK, WIDE)
    theirs_ref[...] = dot_f32(all_ref[...], select_ref[:, WIDE:]).astype(jnp.bfloat16).reshape(4, TOK, WIDE)


def spread(factor, table):
    high = factor.astype(jnp.bfloat16)
    low = (factor - high.astype(jnp.float32)).astype(jnp.bfloat16)
    return dot_f32(high, table) + dot_f32(low, table)


def merge(first, second, table):
    one, two = first.astype(jnp.float32), second.astype(jnp.float32)
    s1, s2 = one[:, 256:], two[:, 256:]
    top = jnp.maximum(s1, s2)
    joined = one * spread(jnp.exp2(s1 - top), table) + two * spread(jnp.exp2(s2 - top), table)
    return joined, top


def merge_cores_kernel(place_ref, mine_ref, got_ref, table_ref, out_ref):
    lanes = lax.broadcasted_iota(jnp.int32, (TOK, 128), 1)
    for r in range(4):
        joined, top = merge(mine_ref[r], got_ref[r ^ 1], table_ref[0])
        tail = joined[:, 256:]
        high = tail.astype(jnp.bfloat16).astype(jnp.float32)
        tail = jnp.where(lanes >= 80, tail + pltpu.roll(tail - high, 8, 1), high)
        tail = jnp.where((lanes >= 64) & (lanes < 72), top, tail)
        to = place_ref[0] ^ (r // 2)
        out_ref[to, r % 2, :, 0:256] = joined[:, :256].astype(jnp.bfloat16)
        out_ref[to, r % 2, :, 256:384] = tail.astype(jnp.bfloat16)


def merge_last_kernel(both_ref, table_ref, out_ref):
    lanes = lax.broadcasted_iota(jnp.int32, (TOK, 128), 1)
    ends = []
    for r in range(2):
        joined, top = merge(both_ref[0, r], both_ref[1, r], table_ref[0])
        tail = joined[:, 256:]
        total = tail + pltpu.roll(tail, 120, 1)
        used = (lanes >= 72) & (lanes < 72 + HEADS_HERE)
        inverse = jnp.where(used, 1.0 / jnp.where(used, total, 1.0), 0.0)
        done = joined * spread(inverse, table_ref[1])
        out_ref[:, r * 256 : (r + 1) * 256] = done[:, :256].astype(jnp.bfloat16)
        ends.append(done[:, 256:])
    out_ref[:, 512:640] = jnp.where(lanes < 64, ends[0], pltpu.roll(ends[1], 64, 1)).astype(jnp.bfloat16)


def project_kernel(place_ref, all_ref, w_ref, keep_ref, send_ref):
    side = place_ref[0]
    here = jnp.zeros((2 * TOK, FEAT), jnp.float32)
    there = jnp.zeros((2 * TOK, FEAT), jnp.float32)
    for near in range(2):
        for odd in range(2):
            rows = all_ref[2 * near + odd]
            ends = rows[:, 512:640]
            turned = pltpu.roll(ends.astype(jnp.float32), 64, 1).astype(jnp.bfloat16)
            wide = jnp.concatenate([rows[:, 0:256], rows[:, 256:512]], axis=0)
            narrow = jnp.concatenate([ends[:, 0:64], turned[:, 0:64]], axis=0)
            w_here = w_ref.at[2 * side + near, odd]
            w_there = w_ref.at[3 - 2 * side - near, odd]
            here = here + dot_f32(wide, w_here[0:256]) + dot_f32(narrow, w_here[256:320])
            there = there + dot_f32(wide, w_there[0:256]) + dot_f32(narrow, w_there[256:320])
    keep_ref[0] = here[0:TOK]
    keep_ref[1] = there[0:TOK]
    send_ref[0] = here[TOK:].astype(jnp.bfloat16)
    send_ref[1] = there[TOK:].astype(jnp.bfloat16)


VMEM = pl.BlockSpec(memory_space=pltpu.VMEM)
SMEM = pl.BlockSpec(memory_space=pltpu.SMEM)
PARAMS = pltpu.CompilerParams(vmem_limit_bytes=40 * 1024 * 1024)


def bf16(*shape):
    return jax.ShapeDtypeStruct(shape, jnp.bfloat16)


def on_device(query, key, value, latents, out_weight, level_gate, levels, frame_mask, seed_block):
    x, y = lax.axis_index("x"), lax.axis_index("y")
    zh, c, zl = lax.axis_index("zh"), lax.axis_index("c"), lax.axis_index("zl")
    column = 4 * x + y

    valid = x // 2 == zl // 4
    w_one = move(
        out_weight,
        lambda x, y, h, c, l: (x, y, 1 - h, c, l) if x // 2 == l // 4 else (3 - x, y, h, c, l ^ 4),
    )
    w_two = move(
        out_weight,
        lambda x, y, h, c, l: None if x // 2 == l // 4 else (3 - x, y, 1 - h, c, l ^ 4),
    )
    w_same = jnp.where(valid, out_weight, w_one)
    w_other = jnp.where(valid, w_one, w_two)
    w_pair = jnp.stack([jnp.where(zh == 0, w_same, w_other), jnp.where(zh == 0, w_other, w_same)])
    weight = lax.all_gather(w_pair, ("x", "y"), axis=0).reshape(4, 2, HALF, FEAT)

    flags = jnp.pad(frame_mask.astype(jnp.bfloat16), ((0, 15), (0, FEAT - 16)))
    q_own = jnp.concatenate([query, flags], axis=0)
    q_far = move(q_own, lambda x, y, h, c, l: (x, y, 1 - h, c, l))
    qa = jnp.stack([q_own, q_far])
    qb = move(qa, lambda x, y, h, c, l: (x, y, h, 1 - c, l))

    kv0 = jnp.stack([key, value])
    kv4 = move(kv0, lambda x, y, h, c, l: ((x + 1) % 4, y, h, c, l))
    kv1 = move(jnp.where(y == 3, kv4, kv0), lambda x, y, h, c, l: (x, (y + 1) % 4, h, c, l))
    kv3 = move(jnp.where(y == 0, kv0, kv4), lambda x, y, h, c, l: (x, (y - 1) % 4, h, c, l))
    kv2 = move(jnp.where(y >= 2, kv4, kv0), lambda x, y, h, c, l: (x, (y + 2) % 4, h, c, l))

    r = jnp.arange(4, dtype=jnp.int32)[:, None]
    d = jnp.arange(5, dtype=jnp.int32)[None, :]
    inner = 2 * (zh ^ (r >> 1)) + (c ^ (r & 1))
    lag = 4 * d + inner - (2 * zh + c)
    age = (4 * column + inner - seed_block[0] - 1) % 64
    code = jnp.where((lag == 0) | ((lag > 0) & (lag <= 16) & (lag <= age)), lag, -1).astype(jnp.int32)

    select = lax.dynamic_index_in_dim(jnp.asarray(SELECTION, jnp.bfloat16), c, keepdims=False)
    table = lax.dynamic_index_in_dim(jnp.asarray(SPREAD, jnp.bfloat16), c, keepdims=False)

    mine, theirs = pl.pallas_call(
        attend_kernel,
        out_shape=(bf16(4, TOK, WIDE), bf16(4, TOK, WIDE)),
        in_specs=[SMEM] + [VMEM] * 8,
        out_specs=(VMEM, VMEM),
        scratch_shapes=[pltpu.VMEM((4 * TOK, FEAT + 128), jnp.bfloat16)],
        compiler_params=PARAMS,
        name="attend",
    )(code, qa, qb, kv0, kv1, kv2, kv3, kv4, select)
    got = move(theirs, lambda x, y, h, c, l: (x, y, h, 1 - c, l))
    both = pl.pallas_call(
        merge_cores_kernel,
        out_shape=bf16(2, 2, TOK, WIDE),
        in_specs=[SMEM] + [VMEM] * 3,
        out_specs=VMEM,
        compiler_params=PARAMS,
        name="merge_cores",
    )(zh.reshape(1), mine, got, table)
    both = lax.all_to_all(both, "zh", 0, 0, tiled=True)
    attended = pl.pallas_call(
        merge_last_kernel,
        out_shape=bf16(TOK, FEAT),
        in_specs=[VMEM] * 2,
        out_specs=VMEM,
        compiler_params=PARAMS,
        name="merge_last",
    )(both, table)
    attended = lax.all_gather(attended, "zl", axis=0, axis_index_groups=[[0, 1, 2, 3], [4, 5, 6, 7]])

    keep, send = pl.pallas_call(
        project_kernel,
        out_shape=(jax.ShapeDtypeStruct((2, TOK, FEAT), jnp.float32), bf16(2, TOK, FEAT)),
        in_specs=[SMEM] + [VMEM] * 2,
        out_specs=(VMEM, VMEM),
        compiler_params=PARAMS,
        name="project",
    )((zl // 4).reshape(1), attended, weight)
    got = move(send, lambda x, y, h, c, l: (x, y, h, 1 - c, l))
    summed = keep + got.astype(jnp.float32)
    far = move(summed[1].astype(jnp.bfloat16), lambda x, y, h, c, l: (x, y, h, c, l ^ 4))

    level_pick = (jnp.arange(LEVELS, dtype=jnp.int32) == levels[0]).astype(jnp.float32)
    gate_row = jnp.sum(level_pick[:, None] * level_gate, axis=0)
    projected = summed[0] + far.astype(jnp.float32)
    return (latents.astype(jnp.float32) + gate_row[None, :] * projected).astype(jnp.bfloat16)


def solution(mesh):
    fine = Mesh(mesh.devices.reshape(SIZES), AXES)
    win = ("x", "y", "zh", "c")
    in_specs = (
        P(win, "zl"),
        P(win, "zl"),
        P(win, "zl"),
        P(win, "zl"),
        P(win, "zl"),
        P(None, "zl"),
        P(win),
        P(win, None),
        P(),
    )
    return jax.shard_map(
        on_device, mesh=fine, in_specs=in_specs, out_specs=P(win, "zl"), check_vma=False
    )
```

```python
import jax
import jax.numpy as jnp
import numpy as np
from jax import lax
from jax.experimental import pallas as pl
from jax.experimental.pallas import tpu as pltpu
from jax.sharding import Mesh, PartitionSpec as P

HD = 128
TOK = 128
LEVELS = 8
HEADS_HERE = 5
FEAT = 640
HALF = 320
WIDE = 384
HIDDEN = -(2.0**100)
SCORE_SCALE = 1.4426950408889634 * HD**-0.5
AXES = ("x", "y", "zh", "c", "zl")
SIZES = (4, 4, 2, 2, 8)


def move(value, rule):
    pairs = []
    for source, place in enumerate(np.ndindex(*SIZES)):
        target = rule(*place)
        if target is not None:
            pairs.append((source, int(np.ravel_multi_index(target, SIZES))))
    return lax.ppermute(value, AXES, pairs)


def half_of_feature(half, lane):
    return (2 * (lane // 80) + half) * 80 + lane % 80


def selection_tables():
    tables = np.zeros((2, 768, 768), np.float32)
    for mine in range(2):
        for slot, half in enumerate((mine, 1 - mine)):
            base = slot * WIDE
            for lane in range(HALF):
                tables[mine, half_of_feature(half, lane), base + lane] = 1
            for stat in range(24):
                tables[mine, FEAT + stat, base + HALF + stat] = 1
    return tables


def spread_tables():
    tables = np.zeros((2, 2, 128, WIDE), np.float32)
    for half in range(2):
        for lane in range(HALF):
            head = half_of_feature(half, lane) // HD
            tables[half, 0, 64 + head, lane] = 1
            tables[half, 1, 72 + head, lane] = 1
        for head in range(HEADS_HERE):
            tables[half, 0, 64 + head, HALF + 8 + head] = 1
            tables[half, 0, 64 + head, HALF + 16 + head] = 1
    return tables


SELECTION = selection_tables()
SPREAD = spread_tables()


def dot_f32(a, b):
    return jnp.dot(a, b, preferred_element_type=jnp.float32)


def pack_kernel(query_ref, mask_ref, out_ref):
    for h in range(HEADS_HERE):
        out_ref[h * HD : (h + 1) * HD, :] = query_ref[:, h * HD : (h + 1) * HD]
    out_ref[FEAT : FEAT + 16, :] = jnp.zeros((16, HD), jnp.bfloat16)
    flags = jnp.broadcast_to(mask_ref[...].astype(jnp.float32), (16, 16))
    out_ref[FEAT : FEAT + 16, 0:16] = flags.astype(jnp.bfloat16)


def attend_kernel(code_ref, qa_ref, qb_ref, *refs):
    kv_refs = refs[0:5]
    select_ref, mine_ref, theirs_ref, all_ref = refs[5:]
    lane = lax.broadcasted_iota(jnp.int32, (1, 128), 1)
    lanes = lax.broadcasted_iota(jnp.int32, (TOK, 128), 1)
    biases = []
    for r in range(4):
        q_ref = qa_ref if r % 2 == 0 else qb_ref
        flags = q_ref[r // 2, FEAT : FEAT + 16].astype(jnp.float32)[0:1]
        row = []
        for d in range(5):
            code = code_ref[r, d]
            hit = jnp.sum(jnp.where(lane == code - 1, flags, 0.0), axis=1, keepdims=True)
            hit = jnp.where(code == 0, 1.0, hit)
            row.append(jnp.broadcast_to(jnp.where(hit > 0.5, 0.0, HIDDEN), (1, 128)))
        biases.append(jnp.concatenate(row, axis=1))
    stats = [jnp.zeros((TOK, 128), jnp.float32) for r in range(4)]
    for h in range(HEADS_HERE):
        cols = slice(h * HD, (h + 1) * HD)
        keys = jnp.concatenate([ref[0, :, cols] for ref in kv_refs], axis=0)
        values = jnp.concatenate([ref[1, :, cols] for ref in kv_refs], axis=0)
        queries = jnp.concatenate(
            [(qa_ref if r % 2 == 0 else qb_ref)[r // 2, cols, :] for r in range(4)], axis=0
        )
        scores = lax.dot_general(queries, keys, (((1,), (1,)), ((), ())), preferred_element_type=jnp.float32)
        parts = []
        for r in range(4):
            part = scores[r * TOK : (r + 1) * TOK] * SCORE_SCALE + biases[r]
            top = jnp.max(part, axis=1, keepdims=True).astype(jnp.bfloat16).astype(jnp.float32)
            expo = jnp.exp2(part - top)
            total = jnp.sum(expo, axis=1, keepdims=True)
            total_hi = total.astype(jnp.bfloat16).astype(jnp.float32)
            parts.append(expo.astype(jnp.bfloat16))
            stats[r] = jnp.where(lanes == h, top, stats[r])
            stats[r] = jnp.where(lanes == 8 + h, total_hi, stats[r])
            stats[r] = jnp.where(lanes == 16 + h, total - total_hi, stats[r])
        summed = dot_f32(jnp.concatenate(parts, axis=0), values)
        all_ref[:, cols] = summed.astype(jnp.bfloat16)
    for r in range(4):
        all_ref[r * TOK : (r + 1) * TOK, FEAT:] = stats[r].astype(jnp.bfloat16)
    mine_ref[...] = dot_f32(all_ref[...], select_ref[:, :WIDE]).astype(jnp.bfloat16).reshape(4, TOK, WIDE)
    theirs_ref[...] = dot_f32(all_ref[...], select_ref[:, WIDE:]).astype(jnp.bfloat16).reshape(4, TOK, WIDE)


def spread(factor, table):
    high = factor.astype(jnp.bfloat16)
    low = (factor - high.astype(jnp.float32)).astype(jnp.bfloat16)
    return dot_f32(high, table) + dot_f32(low, table)


def merge(first, second, table):
    one, two = first.astype(jnp.float32), second.astype(jnp.float32)
    s1, s2 = one[:, 256:], two[:, 256:]
    top = jnp.maximum(s1, s2)
    joined = one * spread(jnp.exp2(s1 - top), table) + two * spread(jnp.exp2(s2 - top), table)
    return joined, top


def merge_cores_kernel(mine_ref, got_ref, table_ref, keep_ref, send_ref):
    lanes = lax.broadcasted_iota(jnp.int32, (TOK, 128), 1)
    for r in range(4):
        joined, top = merge(mine_ref[r], got_ref[r ^ 1], table_ref[0])
        tail = joined[:, 256:]
        high = tail.astype(jnp.bfloat16).astype(jnp.float32)
        tail = jnp.where(lanes >= 80, tail + pltpu.roll(tail - high, 8, 1), high)
        tail = jnp.where((lanes >= 64) & (lanes < 72), top, tail)
        out_ref = keep_ref if r < 2 else send_ref
        out_ref[r % 2, :, 0:256] = joined[:, :256].astype(jnp.bfloat16)
        out_ref[r % 2, :, 256:384] = tail.astype(jnp.bfloat16)


def merge_last_kernel(keep_ref, got_ref, table_ref, out_ref):
    lanes = lax.broadcasted_iota(jnp.int32, (TOK, 128), 1)
    ends = []
    for r in range(2):
        joined, top = merge(keep_ref[r], got_ref[r], table_ref[0])
        tail = joined[:, 256:]
        total = tail + pltpu.roll(tail, 120, 1)
        used = (lanes >= 72) & (lanes < 72 + HEADS_HERE)
        inverse = jnp.where(used, 1.0 / jnp.where(used, total, 1.0), 0.0)
        done = joined * spread(inverse, table_ref[1])
        out_ref[:, r * 256 : (r + 1) * 256] = done[:, :256].astype(jnp.bfloat16)
        ends.append(done[:, 256:])
    out_ref[:, 512:640] = jnp.where(lanes < 64, ends[0], pltpu.roll(ends[1], 64, 1)).astype(jnp.bfloat16)


def project_kernel(place_ref, all_ref, w_ref, keep_ref, send_ref):
    side = place_ref[0]
    here = jnp.zeros((2 * TOK, FEAT), jnp.float32)
    there = jnp.zeros((2 * TOK, FEAT), jnp.float32)
    for near in range(2):
        for odd in range(2):
            rows = all_ref[2 * near + odd]
            ends = rows[:, 512:640]
            turned = pltpu.roll(ends.astype(jnp.float32), 64, 1).astype(jnp.bfloat16)
            wide = jnp.concatenate([rows[:, 0:256], rows[:, 256:512]], axis=0)
            narrow = jnp.concatenate([ends[:, 0:64], turned[:, 0:64]], axis=0)
            w_here = w_ref.at[2 * side + near, odd]
            w_there = w_ref.at[3 - 2 * side - near, odd]
            here = here + dot_f32(wide, w_here[0:256]) + dot_f32(narrow, w_here[256:320])
            there = there + dot_f32(wide, w_there[0:256]) + dot_f32(narrow, w_there[256:320])
    keep_ref[0] = here[0:TOK]
    keep_ref[1] = there[0:TOK]
    send_ref[0] = here[TOK:].astype(jnp.bfloat16)
    send_ref[1] = there[TOK:].astype(jnp.bfloat16)


VMEM = pl.BlockSpec(memory_space=pltpu.VMEM)
SMEM = pl.BlockSpec(memory_space=pltpu.SMEM)
PARAMS = pltpu.CompilerParams(vmem_limit_bytes=40 * 1024 * 1024)


def bf16(*shape):
    return jax.ShapeDtypeStruct(shape, jnp.bfloat16)


def on_device(query, key, value, latents, out_weight, level_gate, levels, frame_mask, seed_block):
    x, y = lax.axis_index("x"), lax.axis_index("y")
    zh, c, zl = lax.axis_index("zh"), lax.axis_index("c"), lax.axis_index("zl")
    column = 4 * x + y

    def behind(own):
        far = move(own, lambda x, y, h, c, l: ((x + 1) % 4, y, h, c, l))
        one = move(jnp.where(y == 3, far, own), lambda x, y, h, c, l: (x, (y + 1) % 4, h, c, l))
        three = move(jnp.where(y == 0, own, far), lambda x, y, h, c, l: (x, (y - 1) % 4, h, c, l))
        two = move(jnp.where(y >= 2, far, own), lambda x, y, h, c, l: (x, (y + 2) % 4, h, c, l))
        return (own, one, two, three, far)

    kvs = behind(jnp.stack([key, value]))
    keys = kvs

    q_own = pl.pallas_call(
        pack_kernel,
        out_shape=bf16(FEAT + 16, HD),
        in_specs=[VMEM] * 2,
        out_specs=VMEM,
        name="pack",
    )(query, frame_mask)
    q_far = move(q_own, lambda x, y, h, c, l: (x, y, 1 - h, c, l))
    qa = jnp.stack([q_own, q_far])
    qb = move(qa, lambda x, y, h, c, l: (x, y, h, 1 - c, l))

    valid = x // 2 == zl // 4
    w_one = move(
        out_weight,
        lambda x, y, h, c, l: (x, y, 1 - h, c, l) if x // 2 == l // 4 else (3 - x, y, h, c, l ^ 4),
    )
    w_two = move(
        out_weight,
        lambda x, y, h, c, l: None if x // 2 == l // 4 else (3 - x, y, 1 - h, c, l ^ 4),
    )
    w_same = jnp.where(valid, out_weight, w_one)
    w_other = jnp.where(valid, w_one, w_two)
    w_pair = jnp.stack([jnp.where(zh == 0, w_same, w_other), jnp.where(zh == 0, w_other, w_same)])
    w_pair, *unused = lax.optimization_barrier((w_pair, kvs[1], kvs[2], kvs[3], q_far))
    weight = lax.all_gather(w_pair, ("x", "y"), axis=0).reshape(4, 2, HALF, FEAT)

    r = jnp.arange(4, dtype=jnp.int32)[:, None]
    d = jnp.arange(5, dtype=jnp.int32)[None, :]
    inner = 2 * (zh ^ (r >> 1)) + (c ^ (r & 1))
    lag = 4 * d + inner - (2 * zh + c)
    age = (4 * column + inner - seed_block[0] - 1) % 64
    code = jnp.where((lag == 0) | ((lag > 0) & (lag <= 16) & (lag <= age)), lag, -1).astype(jnp.int32)

    select = lax.dynamic_index_in_dim(jnp.asarray(SELECTION, jnp.bfloat16), c, keepdims=False)
    table = lax.dynamic_index_in_dim(jnp.asarray(SPREAD, jnp.bfloat16), c, keepdims=False)

    mine, theirs = pl.pallas_call(
        attend_kernel,
        out_shape=(bf16(4, TOK, WIDE), bf16(4, TOK, WIDE)),
        in_specs=[SMEM] + [VMEM] * 8,
        out_specs=(VMEM, VMEM),
        scratch_shapes=[pltpu.VMEM((4 * TOK, FEAT + 128), jnp.bfloat16)],
        compiler_params=PARAMS,
        name="attend",
    )(code, qa, qb, *kvs, select)
    got = move(theirs, lambda x, y, h, c, l: (x, y, h, 1 - c, l))
    keep, send = pl.pallas_call(
        merge_cores_kernel,
        out_shape=(bf16(2, TOK, WIDE), bf16(2, TOK, WIDE)),
        in_specs=[VMEM] * 3,
        out_specs=(VMEM, VMEM),
        compiler_params=PARAMS,
        name="merge_cores",
    )(mine, got, table)
    got = move(send, lambda x, y, h, c, l: (x, y, 1 - h, c, l))
    attended = pl.pallas_call(
        merge_last_kernel,
        out_shape=bf16(TOK, FEAT),
        in_specs=[VMEM] * 3,
        out_specs=VMEM,
        compiler_params=PARAMS,
        name="merge_last",
    )(keep, got, table)
    attended = lax.all_gather(attended, "zl", axis=0, axis_index_groups=[[0, 1, 2, 3], [4, 5, 6, 7]])

    keep, send = pl.pallas_call(
        project_kernel,
        out_shape=(jax.ShapeDtypeStruct((2, TOK, FEAT), jnp.float32), bf16(2, TOK, FEAT)),
        in_specs=[SMEM] + [VMEM] * 2,
        out_specs=(VMEM, VMEM),
        compiler_params=PARAMS,
        name="project",
    )((zl // 4).reshape(1), attended, weight)
    got = move(send, lambda x, y, h, c, l: (x, y, h, 1 - c, l))
    summed = keep + got.astype(jnp.float32)
    far = move(summed[1].astype(jnp.bfloat16), lambda x, y, h, c, l: (x, y, h, c, l ^ 4))

    level_pick = (jnp.arange(LEVELS, dtype=jnp.int32) == levels[0]).astype(jnp.float32)
    gate_row = jnp.sum(level_pick[:, None] * level_gate, axis=0)
    projected = summed[0] + far.astype(jnp.float32)
    return (latents.astype(jnp.float32) + gate_row[None, :] * projected).astype(jnp.bfloat16)


def solution(mesh):
    fine = Mesh(mesh.devices.reshape(SIZES), AXES)
    win = ("x", "y", "zh", "c")
    in_specs = (
        P(win, "zl"),
        P(win, "zl"),
        P(win, "zl"),
        P(win, "zl"),
        P(win, "zl"),
        P(None, "zl"),
        P(win),
        P(win, None),
        P(),
    )
    return jax.shard_map(
        on_device, mesh=fine, in_specs=in_specs, out_specs=P(win, "zl"), check_vma=False
    )
```

```python
import jax
import jax.numpy as jnp
import numpy as np
from jax import lax
from jax.experimental import pallas as pl
from jax.experimental.pallas import tpu as pltpu
from jax.sharding import Mesh, PartitionSpec as P

HD = 128
TOK = 128
LEVELS = 8
HEADS_HERE = 5
FEAT = 640
HALF = 320
WIDE = 384
HIDDEN = -(2.0**100)
SCORE_SCALE = 1.4426950408889634 * HD**-0.5
AXES = ("x", "y", "zh", "c", "zl")
SIZES = (4, 4, 2, 2, 8)


def move(value, rule):
    pairs = []
    for source, place in enumerate(np.ndindex(*SIZES)):
        target = rule(*place)
        if target is not None:
            pairs.append((source, int(np.ravel_multi_index(target, SIZES))))
    return lax.ppermute(value, AXES, pairs)


def half_of_feature(half, lane):
    return (2 * (lane // 80) + half) * 80 + lane % 80


def selection_tables():
    tables = np.zeros((2, 768, 768), np.float32)
    for mine in range(2):
        for slot, half in enumerate((mine, 1 - mine)):
            base = slot * WIDE
            for lane in range(HALF):
                tables[mine, half_of_feature(half, lane), base + lane] = 1
            for stat in range(24):
                tables[mine, FEAT + stat, base + HALF + stat] = 1
    return tables


def spread_tables():
    tables = np.zeros((2, 2, 128, WIDE), np.float32)
    for half in range(2):
        for lane in range(HALF):
            head = half_of_feature(half, lane) // HD
            tables[half, 0, 64 + head, lane] = 1
            tables[half, 1, 72 + head, lane] = 1
        for head in range(HEADS_HERE):
            tables[half, 0, 64 + head, HALF + 8 + head] = 1
            tables[half, 0, 64 + head, HALF + 16 + head] = 1
    return tables


SELECTION = selection_tables()
SPREAD = spread_tables()


def dot_f32(a, b):
    return jnp.dot(a, b, preferred_element_type=jnp.float32)


def pack_kernel(query_ref, mask_ref, out_ref):
    out_ref[0:TOK, :] = query_ref[...]
    out_ref[TOK : TOK + 16, :] = jnp.zeros((16, FEAT), jnp.bfloat16)
    flags = jnp.broadcast_to(mask_ref[...].astype(jnp.float32), (16, 16))
    out_ref[TOK : TOK + 16, 0:16] = flags.astype(jnp.bfloat16)


def attend_kernel(code_ref, qa_ref, qb_ref, own_ref, row_ref, far_ref, select_ref, mine_ref, theirs_ref, all_ref):
    row = code_ref[4, 0]
    kv_refs = [own_ref] + [row_ref.at[(row + 4 - d) % 4] for d in (1, 2, 3)] + [far_ref]
    lane = lax.broadcasted_iota(jnp.int32, (1, 128), 1)
    lanes = lax.broadcasted_iota(jnp.int32, (TOK, 128), 1)
    biases = []
    for r in range(4):
        q_ref = qa_ref if r % 2 == 0 else qb_ref
        flags = q_ref[r // 2, TOK : TOK + 16, 0:HD].astype(jnp.float32)[0:1]
        row = []
        for d in range(5):
            code = code_ref[r, d]
            hit = jnp.sum(jnp.where(lane == code - 1, flags, 0.0), axis=1, keepdims=True)
            hit = jnp.where(code == 0, 1.0, hit)
            row.append(jnp.broadcast_to(jnp.where(hit > 0.5, 0.0, HIDDEN), (1, 128)))
        biases.append(jnp.concatenate(row, axis=1))
    stats = [jnp.zeros((TOK, 128), jnp.float32) for r in range(4)]
    for h in range(HEADS_HERE):
        cols = slice(h * HD, (h + 1) * HD)
        keys = jnp.concatenate([ref[0, :, cols] for ref in kv_refs], axis=0)
        values = jnp.concatenate([ref[1, :, cols] for ref in kv_refs], axis=0)
        queries = jnp.concatenate(
            [(qa_ref if r % 2 == 0 else qb_ref)[r // 2, 0:TOK, cols] for r in range(4)], axis=0
        )
        scores = lax.dot_general(queries, keys, (((1,), (1,)), ((), ())), preferred_element_type=jnp.float32)
        parts = []
        for r in range(4):
            part = scores[r * TOK : (r + 1) * TOK] * SCORE_SCALE + biases[r]
            top = jnp.max(part, axis=1, keepdims=True).astype(jnp.bfloat16).astype(jnp.float32)
            expo = jnp.exp2(part - top)
            total = jnp.sum(expo, axis=1, keepdims=True)
            total_hi = total.astype(jnp.bfloat16).astype(jnp.float32)
            parts.append(expo.astype(jnp.bfloat16))
            stats[r] = jnp.where(lanes == h, top, stats[r])
            stats[r] = jnp.where(lanes == 8 + h, total_hi, stats[r])
            stats[r] = jnp.where(lanes == 16 + h, total - total_hi, stats[r])
        summed = dot_f32(jnp.concatenate(parts, axis=0), values)
        all_ref[:, cols] = summed.astype(jnp.bfloat16)
    for r in range(4):
        all_ref[r * TOK : (r + 1) * TOK, FEAT:] = stats[r].astype(jnp.bfloat16)
    mine_ref[...] = dot_f32(all_ref[...], select_ref[:, :WIDE]).astype(jnp.bfloat16).reshape(4, TOK, WIDE)
    theirs_ref[...] = dot_f32(all_ref[...], select_ref[:, WIDE:]).astype(jnp.bfloat16).reshape(4, TOK, WIDE)


def spread(factor, table):
    high = factor.astype(jnp.bfloat16)
    low = (factor - high.astype(jnp.float32)).astype(jnp.bfloat16)
    return dot_f32(high, table) + dot_f32(low, table)


def merge(first, second, table):
    one, two = first.astype(jnp.float32), second.astype(jnp.float32)
    s1, s2 = one[:, 256:], two[:, 256:]
    top = jnp.maximum(s1, s2)
    joined = one * spread(jnp.exp2(s1 - top), table) + two * spread(jnp.exp2(s2 - top), table)
    return joined, top


def merge_cores_kernel(mine_ref, got_ref, table_ref, keep_ref, send_ref):
    lanes = lax.broadcasted_iota(jnp.int32, (TOK, 128), 1)
    for r in range(4):
        joined, top = merge(mine_ref[r], got_ref[r ^ 1], table_ref[0])
        tail = joined[:, 256:]
        high = tail.astype(jnp.bfloat16).astype(jnp.float32)
        tail = jnp.where(lanes >= 80, tail + pltpu.roll(tail - high, 8, 1), high)
        tail = jnp.where((lanes >= 64) & (lanes < 72), top, tail)
        out_ref = keep_ref if r < 2 else send_ref
        out_ref[r % 2, :, 0:256] = joined[:, :256].astype(jnp.bfloat16)
        out_ref[r % 2, :, 256:384] = tail.astype(jnp.bfloat16)


def merge_last_kernel(keep_ref, got_ref, table_ref, out_ref):
    lanes = lax.broadcasted_iota(jnp.int32, (TOK, 128), 1)
    ends = []
    for r in range(2):
        joined, top = merge(keep_ref[r], got_ref[r], table_ref[0])
        tail = joined[:, 256:]
        total = tail + pltpu.roll(tail, 120, 1)
        used = (lanes >= 72) & (lanes < 72 + HEADS_HERE)
        inverse = jnp.where(used, 1.0 / jnp.where(used, total, 1.0), 0.0)
        done = joined * spread(inverse, table_ref[1])
        out_ref[:, r * 256 : (r + 1) * 256] = done[:, :256].astype(jnp.bfloat16)
        ends.append(done[:, 256:])
    out_ref[:, 512:640] = jnp.where(lanes < 64, ends[0], pltpu.roll(ends[1], 64, 1)).astype(jnp.bfloat16)


def project_kernel(place_ref, all_ref, w_ref, keep_ref, send_ref):
    side = place_ref[0]
    here = jnp.zeros((2 * TOK, FEAT), jnp.float32)
    there = jnp.zeros((2 * TOK, FEAT), jnp.float32)
    for near in range(2):
        for odd in range(2):
            rows = all_ref[2 * near + odd]
            ends = rows[:, 512:640]
            turned = pltpu.roll(ends.astype(jnp.float32), 64, 1).astype(jnp.bfloat16)
            wide = jnp.concatenate([rows[:, 0:256], rows[:, 256:512]], axis=0)
            narrow = jnp.concatenate([ends[:, 0:64], turned[:, 0:64]], axis=0)
            w_here = w_ref.at[2 * side + near, odd]
            w_there = w_ref.at[3 - 2 * side - near, odd]
            here = here + dot_f32(wide, w_here[0:256]) + dot_f32(narrow, w_here[256:320])
            there = there + dot_f32(wide, w_there[0:256]) + dot_f32(narrow, w_there[256:320])
    keep_ref[0] = here[0:TOK]
    keep_ref[1] = there[0:TOK]
    send_ref[0] = here[TOK:].astype(jnp.bfloat16)
    send_ref[1] = there[TOK:].astype(jnp.bfloat16)


VMEM = pl.BlockSpec(memory_space=pltpu.VMEM)
SMEM = pl.BlockSpec(memory_space=pltpu.SMEM)
PARAMS = pltpu.CompilerParams(vmem_limit_bytes=40 * 1024 * 1024)
ROOMY = pltpu.CompilerParams(vmem_limit_bytes=60 * 1024 * 1024)


def bf16(*shape):
    return jax.ShapeDtypeStruct(shape, jnp.bfloat16)


def on_device(query, key, value, latents, out_weight, level_gate, levels, frame_mask, seed_block):
    x, y = lax.axis_index("x"), lax.axis_index("y")
    zh, c, zl = lax.axis_index("zh"), lax.axis_index("c"), lax.axis_index("zl")
    column = 4 * x + y

    kv_own = jnp.stack([key, value])
    kv_far = move(kv_own, lambda x, y, h, c, l: ((x + 1) % 4, y, h, c, l))
    to = jnp.arange(4, dtype=jnp.int32)[:, None, None, None]
    kv_row = lax.all_to_all(jnp.where(to > y, kv_own[None], kv_far[None]), "y", 0, 0, tiled=True)

    w_turned = move(out_weight, lambda x, y, h, c, l: (x, y, h, 1 - c, l))
    w_one = move(
        w_turned,
        lambda x, y, h, c, l: (x, y, 1 - h, 1 - c, l) if x // 2 == l // 4 else (3 - x, y, h, 1 - c, l ^ 4),
    )
    w_two = move(
        w_turned,
        lambda x, y, h, c, l: None if x // 2 == l // 4 else (3 - x, y, 1 - h, 1 - c, l ^ 4),
    )
    valid = x // 2 == zl // 4
    w_same = jnp.where(valid, out_weight, w_one)
    w_other = jnp.where(valid, w_one, w_two)
    w_pair = jnp.stack([jnp.where(zh == 0, w_same, w_other), jnp.where(zh == 0, w_other, w_same)])

    packed = pl.pallas_call(
        pack_kernel,
        out_shape=bf16(TOK + 16, FEAT),
        in_specs=[VMEM] * 2,
        out_specs=VMEM,
        name="pack",
    )(query, frame_mask)
    mate = move(packed, lambda x, y, h, c, l: (x, y, 1 - h, c, l))
    qa = jnp.stack([packed, mate])
    qb = move(qa, lambda x, y, h, c, l: (x, y, h, 1 - c, l))

    r = jnp.arange(4, dtype=jnp.int32)[:, None]
    d = jnp.arange(5, dtype=jnp.int32)[None, :]
    inner = 2 * (zh ^ (r >> 1)) + (c ^ (r & 1))
    lag = 4 * d + inner - (2 * zh + c)
    age = (4 * column + inner - seed_block[0] - 1) % 64
    code = jnp.where((lag == 0) | ((lag > 0) & (lag <= 16) & (lag <= age)), lag, -1).astype(jnp.int32)
    code = jnp.concatenate([code, jnp.broadcast_to(y, (1, 5)).astype(jnp.int32)], axis=0)

    select = lax.dynamic_index_in_dim(jnp.asarray(SELECTION, jnp.bfloat16), c, keepdims=False)
    table = lax.dynamic_index_in_dim(jnp.asarray(SPREAD, jnp.bfloat16), c, keepdims=False)

    weight = lax.all_to_all(jnp.broadcast_to(w_pair[None], (16, 2, 80, FEAT)), ("x", "y"), 0, 0, tiled=True)
    weight = weight.reshape(4, 2, HALF, FEAT)
    mine, theirs = pl.pallas_call(
        attend_kernel,
        out_shape=(bf16(4, TOK, WIDE), bf16(4, TOK, WIDE)),
        in_specs=[SMEM] + [VMEM] * 6,
        out_specs=(VMEM, VMEM),
        scratch_shapes=[pltpu.VMEM((4 * TOK, FEAT + 128), jnp.bfloat16)],
        compiler_params=ROOMY,
        cost_estimate=pl.CostEstimate(flops=60000000000, bytes_accessed=4000000, transcendentals=0),
        name="attend",
    )(code, qa, qb, kv_own, kv_row, kv_far, select)
    got = move(theirs, lambda x, y, h, c, l: (x, y, h, 1 - c, l))
    keep, send = pl.pallas_call(
        merge_cores_kernel,
        out_shape=(bf16(2, TOK, WIDE), bf16(2, TOK, WIDE)),
        in_specs=[VMEM] * 3,
        out_specs=(VMEM, VMEM),
        compiler_params=PARAMS,
        name="merge_cores",
    )(mine, got, table)
    got = move(send, lambda x, y, h, c, l: (x, y, 1 - h, c, l))
    attended = pl.pallas_call(
        merge_last_kernel,
        out_shape=bf16(TOK, FEAT),
        in_specs=[VMEM] * 3,
        out_specs=VMEM,
        compiler_params=PARAMS,
        name="merge_last",
    )(keep, got, table)
    attended = lax.all_gather(attended, "zl", axis=0, axis_index_groups=[[0, 1, 2, 3], [4, 5, 6, 7]])

    keep, send = pl.pallas_call(
        project_kernel,
        out_shape=(jax.ShapeDtypeStruct((2, TOK, FEAT), jnp.float32), bf16(2, TOK, FEAT)),
        in_specs=[SMEM] + [VMEM] * 2,
        out_specs=(VMEM, VMEM),
        compiler_params=PARAMS,
        name="project",
    )((zl // 4).reshape(1), attended, weight)
    got = move(send, lambda x, y, h, c, l: (x, y, h, 1 - c, l))
    summed = keep + got.astype(jnp.float32)
    far = move(summed[1].astype(jnp.bfloat16), lambda x, y, h, c, l: (x, y, h, c, l ^ 4))

    level_pick = (jnp.arange(LEVELS, dtype=jnp.int32) == levels[0]).astype(jnp.float32)
    gate_row = jnp.sum(level_pick[:, None] * level_gate, axis=0)
    projected = summed[0] + far.astype(jnp.float32)
    return (latents.astype(jnp.float32) + gate_row[None, :] * projected).astype(jnp.bfloat16)


def solution(mesh):
    fine = Mesh(mesh.devices.reshape(SIZES), AXES)
    win = ("x", "y", "zh", "c")
    in_specs = (
        P(win, "zl"),
        P(win, "zl"),
        P(win, "zl"),
        P(win, "zl"),
        P(win, "zl"),
        P(None, "zl"),
        P(win),
        P(win, None),
        P(),
    )
    return jax.shard_map(
        on_device, mesh=fine, in_specs=in_specs, out_specs=P(win, "zl"), check_vma=False
    )
```

```python
import functools

import jax
import jax.numpy as jnp
import numpy as np
from jax import lax
from jax.experimental import pallas as pl
from jax.experimental.pallas import tpu as pltpu
from jax.sharding import Mesh, PartitionSpec as P

HD = 128
TOK = 128
LEVELS = 8
HEADS_HERE = 5
FEAT = 640
HALF = 320
WIDE = 384
HIDDEN = -(2.0**100)
SCORE_SCALE = 1.4426950408889634 * HD**-0.5
AXES = ("x", "y", "zh", "c", "zl")
SIZES = (4, 4, 2, 2, 8)


def move(value, rule):
    pairs = []
    for source, place in enumerate(np.ndindex(*SIZES)):
        target = rule(*place)
        if target is not None:
            pairs.append((source, int(np.ravel_multi_index(target, SIZES))))
    return lax.ppermute(value, AXES, pairs)


def half_of_feature(half, lane):
    return (2 * (lane // 80) + half) * 80 + lane % 80


def selection_tables():
    tables = np.zeros((2, 768, 768), np.float32)
    for mine in range(2):
        for slot, half in enumerate((mine, 1 - mine)):
            base = slot * WIDE
            for lane in range(HALF):
                tables[mine, half_of_feature(half, lane), base + lane] = 1
            for stat in range(24):
                tables[mine, FEAT + stat, base + HALF + stat] = 1
    return tables


def spread_tables():
    tables = np.zeros((2, 2, 128, WIDE), np.float32)
    for half in range(2):
        for lane in range(HALF):
            head = half_of_feature(half, lane) // HD
            tables[half, 0, 64 + head, lane] = 1
            tables[half, 1, 72 + head, lane] = 1
        for head in range(HEADS_HERE):
            tables[half, 0, 64 + head, HALF + 8 + head] = 1
            tables[half, 0, 64 + head, HALF + 16 + head] = 1
    return tables


SELECTION = selection_tables()
SPREAD = spread_tables()


def dot_f32(a, b):
    return jnp.dot(a, b, preferred_element_type=jnp.float32)


def pack_kernel(query_ref, mask_ref, out_ref):
    out_ref[0:TOK, :] = query_ref[...]
    out_ref[TOK : TOK + 16, :] = jnp.zeros((16, FEAT), jnp.bfloat16)
    flags = jnp.broadcast_to(mask_ref[...].astype(jnp.float32), (16, 16))
    out_ref[TOK : TOK + 16, 0:16] = flags.astype(jnp.bfloat16)


def attend_kernel(code_ref, qa_ref, qb_ref, own_ref, row_ref, far_ref, select_ref, mine_ref, theirs_ref, all_ref):
    row = code_ref[4, 0]
    kv_refs = [own_ref] + [row_ref.at[(row + 4 - d) % 4] for d in (1, 2, 3)] + [far_ref]
    lane = lax.broadcasted_iota(jnp.int32, (1, 128), 1)
    lanes = lax.broadcasted_iota(jnp.int32, (TOK, 128), 1)
    biases = []
    for r in range(4):
        q_ref = qa_ref if r % 2 == 0 else qb_ref
        flags = q_ref[r // 2, TOK : TOK + 16, 0:HD].astype(jnp.float32)[0:1]
        row = []
        for d in range(5):
            code = code_ref[r, d]
            hit = jnp.sum(jnp.where(lane == code - 1, flags, 0.0), axis=1, keepdims=True)
            hit = jnp.where(code == 0, 1.0, hit)
            row.append(jnp.broadcast_to(jnp.where(hit > 0.5, 0.0, HIDDEN), (1, 128)))
        biases.append(jnp.concatenate(row, axis=1))
    stats = [jnp.zeros((TOK, 128), jnp.float32) for r in range(4)]
    for h in range(HEADS_HERE):
        cols = slice(h * HD, (h + 1) * HD)
        keys = jnp.concatenate([ref[0, :, cols] for ref in kv_refs], axis=0)
        values = jnp.concatenate([ref[1, :, cols] for ref in kv_refs], axis=0)
        queries = jnp.concatenate(
            [(qa_ref if r % 2 == 0 else qb_ref)[r // 2, 0:TOK, cols] for r in range(4)], axis=0
        )
        scores = lax.dot_general(queries, keys, (((1,), (1,)), ((), ())), preferred_element_type=jnp.float32)
        parts = []
        for r in range(4):
            part = scores[r * TOK : (r + 1) * TOK] * SCORE_SCALE + biases[r]
            top = jnp.max(part, axis=1, keepdims=True).astype(jnp.bfloat16).astype(jnp.float32)
            expo = jnp.exp2(part - top)
            total = jnp.sum(expo, axis=1, keepdims=True)
            total_hi = total.astype(jnp.bfloat16).astype(jnp.float32)
            parts.append(expo.astype(jnp.bfloat16))
            stats[r] = jnp.where(lanes == h, top, stats[r])
            stats[r] = jnp.where(lanes == 8 + h, total_hi, stats[r])
            stats[r] = jnp.where(lanes == 16 + h, total - total_hi, stats[r])
        summed = dot_f32(jnp.concatenate(parts, axis=0), values)
        all_ref[:, cols] = summed.astype(jnp.bfloat16)
    for r in range(4):
        all_ref[r * TOK : (r + 1) * TOK, FEAT:] = stats[r].astype(jnp.bfloat16)
    mine_ref[...] = dot_f32(all_ref[...], select_ref[:, :WIDE]).astype(jnp.bfloat16).reshape(4, TOK, WIDE)
    theirs_ref[...] = dot_f32(all_ref[...], select_ref[:, WIDE:]).astype(jnp.bfloat16).reshape(4, TOK, WIDE)


def spread(factor, table):
    high = factor.astype(jnp.bfloat16)
    low = (factor - high.astype(jnp.float32)).astype(jnp.bfloat16)
    return dot_f32(high, table) + dot_f32(low, table)


def merge(first, second, table):
    one, two = first.astype(jnp.float32), second.astype(jnp.float32)
    s1, s2 = one[:, 256:], two[:, 256:]
    top = jnp.maximum(s1, s2)
    joined = one * spread(jnp.exp2(s1 - top), table) + two * spread(jnp.exp2(s2 - top), table)
    return joined, top


def merge_cores_kernel(mine_ref, got_ref, table_ref, keep_ref, send_ref):
    lanes = lax.broadcasted_iota(jnp.int32, (TOK, 128), 1)
    for r in range(4):
        joined, top = merge(mine_ref[r], got_ref[r ^ 1], table_ref[0])
        tail = joined[:, 256:]
        high = tail.astype(jnp.bfloat16).astype(jnp.float32)
        tail = jnp.where(lanes >= 80, tail + pltpu.roll(tail - high, 8, 1), high)
        tail = jnp.where((lanes >= 64) & (lanes < 72), top, tail)
        out_ref = keep_ref if r < 2 else send_ref
        out_ref[r % 2, :, 0:256] = joined[:, :256].astype(jnp.bfloat16)
        out_ref[r % 2, :, 256:384] = tail.astype(jnp.bfloat16)


def merge_last_kernel(keep_ref, got_ref, table_ref, out_ref):
    lanes = lax.broadcasted_iota(jnp.int32, (TOK, 128), 1)
    ends = []
    for r in range(2):
        joined, top = merge(keep_ref[r], got_ref[r], table_ref[0])
        tail = joined[:, 256:]
        total = tail + pltpu.roll(tail, 120, 1)
        used = (lanes >= 72) & (lanes < 72 + HEADS_HERE)
        inverse = jnp.where(used, 1.0 / jnp.where(used, total, 1.0), 0.0)
        done = joined * spread(inverse, table_ref[1])
        out_ref[:, r * 256 : (r + 1) * 256] = done[:, :256].astype(jnp.bfloat16)
        ends.append(done[:, 256:])
    out_ref[:, 512:640] = jnp.where(lanes < 64, ends[0], pltpu.roll(ends[1], 64, 1)).astype(jnp.bfloat16)


def project_kernel(away, place_ref, all_ref, w_ref, keep_ref, send_ref):
    side = place_ref[0]
    total = jnp.zeros((2 * TOK, FEAT), jnp.float32)
    for near in range(2):
        for odd in range(2):
            rows = all_ref[2 * near + odd]
            ends = rows[:, 512:640]
            turned = pltpu.roll(ends.astype(jnp.float32), 64, 1).astype(jnp.bfloat16)
            wide = jnp.concatenate([rows[:, 0:256], rows[:, 256:512]], axis=0)
            narrow = jnp.concatenate([ends[:, 0:64], turned[:, 0:64]], axis=0)
            w_at = w_ref.at[3 - 2 * side - near if away else 2 * side + near, odd]
            total = total + dot_f32(wide, w_at[0:256]) + dot_f32(narrow, w_at[256:320])
    keep_ref[...] = total[0:TOK]
    send_ref[...] = total[TOK:].astype(jnp.bfloat16)


VMEM = pl.BlockSpec(memory_space=pltpu.VMEM)
SMEM = pl.BlockSpec(memory_space=pltpu.SMEM)
PARAMS = pltpu.CompilerParams(vmem_limit_bytes=40 * 1024 * 1024)
ROOMY = pltpu.CompilerParams(vmem_limit_bytes=60 * 1024 * 1024)


def bf16(*shape):
    return jax.ShapeDtypeStruct(shape, jnp.bfloat16)


def on_device(query, key, value, latents, out_weight, level_gate, levels, frame_mask, seed_block):
    x, y = lax.axis_index("x"), lax.axis_index("y")
    zh, c, zl = lax.axis_index("zh"), lax.axis_index("c"), lax.axis_index("zl")
    column = 4 * x + y

    kv_own = jnp.stack([key, value])
    kv_far = move(kv_own, lambda x, y, h, c, l: ((x + 1) % 4, y, h, c, l))
    to = jnp.arange(4, dtype=jnp.int32)[:, None, None, None]
    kv_row = lax.all_to_all(jnp.where(to > y, kv_own[None], kv_far[None]), "y", 0, 0, tiled=True)

    w_turned = move(out_weight, lambda x, y, h, c, l: (x, y, h, 1 - c, l))
    w_one = move(
        w_turned,
        lambda x, y, h, c, l: (x, y, 1 - h, 1 - c, l) if x // 2 == l // 4 else (3 - x, y, h, 1 - c, l ^ 4),
    )
    w_two = move(
        w_turned,
        lambda x, y, h, c, l: None if x // 2 == l // 4 else (3 - x, y, 1 - h, 1 - c, l ^ 4),
    )
    valid = x // 2 == zl // 4
    w_same = jnp.where(valid, out_weight, w_one)
    w_other = jnp.where(valid, w_one, w_two)
    w_pair = jnp.stack([jnp.where(zh == 0, w_same, w_other), jnp.where(zh == 0, w_other, w_same)])

    packed = pl.pallas_call(
        pack_kernel,
        out_shape=bf16(TOK + 16, FEAT),
        in_specs=[VMEM] * 2,
        out_specs=VMEM,
        name="pack",
    )(query, frame_mask)
    mate = move(packed, lambda x, y, h, c, l: (x, y, 1 - h, c, l))
    qa = jnp.stack([packed, mate])
    qb = move(qa, lambda x, y, h, c, l: (x, y, h, 1 - c, l))

    r = jnp.arange(4, dtype=jnp.int32)[:, None]
    d = jnp.arange(5, dtype=jnp.int32)[None, :]
    inner = 2 * (zh ^ (r >> 1)) + (c ^ (r & 1))
    lag = 4 * d + inner - (2 * zh + c)
    age = (4 * column + inner - seed_block[0] - 1) % 64
    code = jnp.where((lag == 0) | ((lag > 0) & (lag <= 16) & (lag <= age)), lag, -1).astype(jnp.int32)
    code = jnp.concatenate([code, jnp.broadcast_to(y, (1, 5)).astype(jnp.int32)], axis=0)

    select = lax.dynamic_index_in_dim(jnp.asarray(SELECTION, jnp.bfloat16), c, keepdims=False)
    table = lax.dynamic_index_in_dim(jnp.asarray(SPREAD, jnp.bfloat16), c, keepdims=False)

    weight = lax.all_to_all(jnp.broadcast_to(w_pair[None], (16, 2, 80, FEAT)), ("x", "y"), 0, 0, tiled=True)
    weight = weight.reshape(4, 2, HALF, FEAT)
    mine, theirs = pl.pallas_call(
        attend_kernel,
        out_shape=(bf16(4, TOK, WIDE), bf16(4, TOK, WIDE)),
        in_specs=[SMEM] + [VMEM] * 6,
        out_specs=(VMEM, VMEM),
        scratch_shapes=[pltpu.VMEM((4 * TOK, FEAT + 128), jnp.bfloat16)],
        compiler_params=ROOMY,
        cost_estimate=pl.CostEstimate(flops=60000000000, bytes_accessed=4000000, transcendentals=0),
        name="attend",
    )(code, qa, qb, kv_own, kv_row, kv_far, select)
    got = move(theirs, lambda x, y, h, c, l: (x, y, h, 1 - c, l))
    keep, send = pl.pallas_call(
        merge_cores_kernel,
        out_shape=(bf16(2, TOK, WIDE), bf16(2, TOK, WIDE)),
        in_specs=[VMEM] * 3,
        out_specs=(VMEM, VMEM),
        compiler_params=PARAMS,
        name="merge_cores",
    )(mine, got, table)
    got = move(send, lambda x, y, h, c, l: (x, y, 1 - h, c, l))
    attended = pl.pallas_call(
        merge_last_kernel,
        out_shape=bf16(TOK, FEAT),
        in_specs=[VMEM] * 3,
        out_specs=VMEM,
        compiler_params=PARAMS,
        name="merge_last",
    )(keep, got, table)
    attended = lax.all_gather(attended, "zl", axis=0, axis_index_groups=[[0, 1, 2, 3], [4, 5, 6, 7]])

    def project(away, attended):
        keep, send = pl.pallas_call(
            functools.partial(project_kernel, away),
            out_shape=(jax.ShapeDtypeStruct((TOK, FEAT), jnp.float32), bf16(TOK, FEAT)),
            in_specs=[SMEM] + [VMEM] * 2,
            out_specs=(VMEM, VMEM),
            compiler_params=PARAMS,
            name="project",
        )((zl // 4).reshape(1), attended, weight)
        got = move(send, lambda x, y, h, c, l: (x, y, h, 1 - c, l))
        return keep + got.astype(jnp.float32)

    there = project(True, attended).astype(jnp.bfloat16)
    far = move(there, lambda x, y, h, c, l: (x, y, h, c, l ^ 4))
    attended, unused = lax.optimization_barrier((attended, there))
    here = project(False, attended)

    level_pick = (jnp.arange(LEVELS, dtype=jnp.int32) == levels[0]).astype(jnp.float32)
    gate_row = jnp.sum(level_pick[:, None] * level_gate, axis=0)
    projected = here + far.astype(jnp.float32)
    return (latents.astype(jnp.float32) + gate_row[None, :] * projected).astype(jnp.bfloat16)


def solution(mesh):
    fine = Mesh(mesh.devices.reshape(SIZES), AXES)
    win = ("x", "y", "zh", "c")
    in_specs = (
        P(win, "zl"),
        P(win, "zl"),
        P(win, "zl"),
        P(win, "zl"),
        P(win, "zl"),
        P(None, "zl"),
        P(win),
        P(win, None),
        P(),
    )
    return jax.shard_map(
        on_device, mesh=fine, in_specs=in_specs, out_specs=P(win, "zl"), check_vma=False
    )
```

```python
import functools

import jax
import jax.numpy as jnp
import numpy as np
from jax import lax
from jax.experimental import pallas as pl
from jax.experimental.pallas import tpu as pltpu
from jax.sharding import Mesh, PartitionSpec as P

HD = 128
TOK = 128
LEVELS = 8
HEADS_HERE = 5
FEAT = 640
HALF = 320
WIDE = 384
HIDDEN = -(2.0**100)
SCORE_SCALE = 1.4426950408889634 * HD**-0.5
AXES = ("x", "y", "zh", "c", "zl")
SIZES = (4, 4, 2, 2, 8)


def move(value, rule):
    pairs = []
    for source, place in enumerate(np.ndindex(*SIZES)):
        target = rule(*place)
        if target is not None:
            pairs.append((source, int(np.ravel_multi_index(target, SIZES))))
    return lax.ppermute(value, AXES, pairs)


def half_of_feature(half, lane):
    return (2 * (lane // 80) + half) * 80 + lane % 80


def selection_tables():
    tables = np.zeros((2, 768, 768), np.float32)
    for mine in range(2):
        for slot, half in enumerate((mine, 1 - mine)):
            base = slot * WIDE
            for lane in range(HALF):
                tables[mine, half_of_feature(half, lane), base + lane] = 1
            for stat in range(24):
                tables[mine, FEAT + stat, base + HALF + stat] = 1
    return tables


def spread_tables():
    tables = np.zeros((2, 2, 128, WIDE), np.float32)
    for half in range(2):
        for lane in range(HALF):
            head = half_of_feature(half, lane) // HD
            tables[half, 0, 64 + head, lane] = 1
            tables[half, 1, 72 + head, lane] = 1
        for head in range(HEADS_HERE):
            tables[half, 0, 64 + head, HALF + 8 + head] = 1
            tables[half, 0, 64 + head, HALF + 16 + head] = 1
    return tables


SELECTION = selection_tables()
SPREAD = spread_tables()


def dot_f32(a, b):
    return jnp.dot(a, b, preferred_element_type=jnp.float32)


def pack_kernel(query_ref, mask_ref, out_ref):
    for h in range(HEADS_HERE):
        out_ref[h * HD : (h + 1) * HD, :] = query_ref[:, h * HD : (h + 1) * HD]
    out_ref[FEAT : FEAT + 16, :] = jnp.zeros((16, HD), jnp.bfloat16)
    flags = jnp.broadcast_to(mask_ref[...].astype(jnp.float32), (16, 16))
    out_ref[FEAT : FEAT + 16, 0:16] = flags.astype(jnp.bfloat16)


def attend_kernel(code_ref, qa_ref, qb_ref, own_ref, row_ref, far_ref, select_ref, mine_ref, theirs_ref, all_ref):
    row = code_ref[4, 0]
    kv_refs = [own_ref] + [row_ref.at[(row + 4 - d) % 4] for d in (1, 2, 3)] + [far_ref]
    lane = lax.broadcasted_iota(jnp.int32, (1, 128), 1)
    lanes = lax.broadcasted_iota(jnp.int32, (TOK, 128), 1)
    biases = []
    for r in range(4):
        q_ref = qa_ref if r % 2 == 0 else qb_ref
        flags = q_ref[r // 2, FEAT : FEAT + 16].astype(jnp.float32)[0:1]
        row = []
        for d in range(5):
            code = code_ref[r, d]
            hit = jnp.sum(jnp.where(lane == code - 1, flags, 0.0), axis=1, keepdims=True)
            hit = jnp.where(code == 0, 1.0, hit)
            row.append(jnp.broadcast_to(jnp.where(hit > 0.5, 0.0, HIDDEN), (1, 128)))
        biases.append(jnp.concatenate(row, axis=1))
    stats = [jnp.zeros((TOK, 128), jnp.float32) for r in range(4)]
    for h in range(HEADS_HERE):
        cols = slice(h * HD, (h + 1) * HD)
        keys = jnp.concatenate([ref[0, :, cols] for ref in kv_refs], axis=0)
        values = jnp.concatenate([ref[1, :, cols] for ref in kv_refs], axis=0)
        queries = jnp.concatenate(
            [(qa_ref if r % 2 == 0 else qb_ref)[r // 2, cols, :] for r in range(4)], axis=0
        )
        scores = lax.dot_general(queries, keys, (((1,), (1,)), ((), ())), preferred_element_type=jnp.float32)
        parts = []
        for r in range(4):
            part = scores[r * TOK : (r + 1) * TOK] * SCORE_SCALE + biases[r]
            top = jnp.max(part, axis=1, keepdims=True).astype(jnp.bfloat16).astype(jnp.float32)
            expo = jnp.exp2(part - top)
            total = jnp.sum(expo, axis=1, keepdims=True)
            total_hi = total.astype(jnp.bfloat16).astype(jnp.float32)
            parts.append(expo.astype(jnp.bfloat16))
            stats[r] = jnp.where(lanes == h, top, stats[r])
            stats[r] = jnp.where(lanes == 8 + h, total_hi, stats[r])
            stats[r] = jnp.where(lanes == 16 + h, total - total_hi, stats[r])
        summed = dot_f32(jnp.concatenate(parts, axis=0), values)
        all_ref[:, cols] = summed.astype(jnp.bfloat16)
    for r in range(4):
        all_ref[r * TOK : (r + 1) * TOK, FEAT:] = stats[r].astype(jnp.bfloat16)
    mine_ref[...] = dot_f32(all_ref[...], select_ref[code_ref[4, 1], :, :WIDE]).astype(jnp.bfloat16).reshape(4, TOK, WIDE)
    theirs_ref[...] = dot_f32(all_ref[...], select_ref[code_ref[4, 1], :, WIDE:]).astype(jnp.bfloat16).reshape(4, TOK, WIDE)


def spread(factor, table):
    high = factor.astype(jnp.bfloat16)
    low = (factor - high.astype(jnp.float32)).astype(jnp.bfloat16)
    return dot_f32(high, table) + dot_f32(low, table)


def merge(first, second, table):
    one, two = first.astype(jnp.float32), second.astype(jnp.float32)
    s1, s2 = one[:, 256:], two[:, 256:]
    top = jnp.maximum(s1, s2)
    joined = one * spread(jnp.exp2(s1 - top), table) + two * spread(jnp.exp2(s2 - top), table)
    return joined, top


def merge_cores_kernel(mine_ref, got_ref, table_ref, keep_ref, send_ref):
    lanes = lax.broadcasted_iota(jnp.int32, (TOK, 128), 1)
    for r in range(4):
        joined, top = merge(mine_ref[r], got_ref[r ^ 1], table_ref[0])
        tail = joined[:, 256:]
        high = tail.astype(jnp.bfloat16).astype(jnp.float32)
        tail = jnp.where(lanes >= 80, tail + pltpu.roll(tail - high, 8, 1), high)
        tail = jnp.where((lanes >= 64) & (lanes < 72), top, tail)
        out_ref = keep_ref if r < 2 else send_ref
        out_ref[r % 2, :, 0:256] = joined[:, :256].astype(jnp.bfloat16)
        out_ref[r % 2, :, 256:384] = tail.astype(jnp.bfloat16)


def merge_last_kernel(keep_ref, got_ref, table_ref, out_ref):
    lanes = lax.broadcasted_iota(jnp.int32, (TOK, 128), 1)
    ends = []
    for r in range(2):
        joined, top = merge(keep_ref[r], got_ref[r], table_ref[0])
        tail = joined[:, 256:]
        total = tail + pltpu.roll(tail, 120, 1)
        used = (lanes >= 72) & (lanes < 72 + HEADS_HERE)
        inverse = jnp.where(used, 1.0 / jnp.where(used, total, 1.0), 0.0)
        done = joined * spread(inverse, table_ref[1])
        out_ref[:, r * 256 : (r + 1) * 256] = done[:, :256].astype(jnp.bfloat16)
        ends.append(done[:, 256:])
    out_ref[:, 512:640] = jnp.where(lanes < 64, ends[0], pltpu.roll(ends[1], 64, 1)).astype(jnp.bfloat16)


def project_kernel(away, place_ref, all_ref, w_ref, keep_ref, send_ref):
    side = place_ref[0]
    total = jnp.zeros((2 * TOK, FEAT), jnp.float32)
    for near in range(2):
        for odd in range(2):
            rows = all_ref[2 * near + odd]
            ends = rows[:, 512:640]
            turned = pltpu.roll(ends.astype(jnp.float32), 64, 1).astype(jnp.bfloat16)
            wide = jnp.concatenate([rows[:, 0:256], rows[:, 256:512]], axis=0)
            narrow = jnp.concatenate([ends[:, 0:64], turned[:, 0:64]], axis=0)
            w_at = w_ref.at[3 - 2 * side - near if away else 2 * side + near, odd]
            total = total + dot_f32(wide, w_at[0:256]) + dot_f32(narrow, w_at[256:320])
    keep_ref[...] = total[0:TOK]
    send_ref[...] = total[TOK:].astype(jnp.bfloat16)


VMEM = pl.BlockSpec(memory_space=pltpu.VMEM)
SMEM = pl.BlockSpec(memory_space=pltpu.SMEM)
PARAMS = pltpu.CompilerParams(vmem_limit_bytes=40 * 1024 * 1024)
ROOMY = pltpu.CompilerParams(vmem_limit_bytes=60 * 1024 * 1024)


def bf16(*shape):
    return jax.ShapeDtypeStruct(shape, jnp.bfloat16)


def on_device(query, key, value, latents, out_weight, level_gate, levels, frame_mask, seed_block):
    x, y = lax.axis_index("x"), lax.axis_index("y")
    zh, c, zl = lax.axis_index("zh"), lax.axis_index("c"), lax.axis_index("zl")
    column = 4 * x + y

    kv_own = jnp.stack([key, value])
    kv_far = move(kv_own, lambda x, y, h, c, l: ((x + 1) % 4, y, h, c, l))
    to = jnp.arange(4, dtype=jnp.int32)[:, None, None, None]
    kv_row = lax.all_to_all(jnp.where(to > y, kv_own[None], kv_far[None]), "y", 0, 0, tiled=True)

    w_turned = move(out_weight, lambda x, y, h, c, l: (x, y, h, 1 - c, l))
    w_one = move(
        w_turned,
        lambda x, y, h, c, l: (x, y, 1 - h, 1 - c, l) if x // 2 == l // 4 else (3 - x, y, h, 1 - c, l ^ 4),
    )
    w_two = move(
        w_turned,
        lambda x, y, h, c, l: None if x // 2 == l // 4 else (3 - x, y, 1 - h, 1 - c, l ^ 4),
    )
    valid = x // 2 == zl // 4
    w_same = jnp.where(valid, out_weight, w_one)
    w_other = jnp.where(valid, w_one, w_two)
    w_pair = jnp.stack([jnp.where(zh == 0, w_same, w_other), jnp.where(zh == 0, w_other, w_same)])

    packed = pl.pallas_call(
        pack_kernel,
        out_shape=bf16(FEAT + 16, HD),
        in_specs=[VMEM] * 2,
        out_specs=VMEM,
        name="pack",
    )(query, frame_mask)
    mate = move(packed, lambda x, y, h, c, l: (x, y, 1 - h, c, l))
    qa = jnp.stack([packed, mate])
    qb = move(qa, lambda x, y, h, c, l: (x, y, h, 1 - c, l))

    r = jnp.arange(4, dtype=jnp.int32)[:, None]
    d = jnp.arange(5, dtype=jnp.int32)[None, :]
    inner = 2 * (zh ^ (r >> 1)) + (c ^ (r & 1))
    lag = 4 * d + inner - (2 * zh + c)
    age = (4 * column + inner - seed_block[0] - 1) % 64
    code = jnp.where((lag == 0) | ((lag > 0) & (lag <= 16) & (lag <= age)), lag, -1).astype(jnp.int32)
    code = jnp.concatenate([code, jnp.stack([y, c, c, c, c])[None].astype(jnp.int32)], axis=0)

    select = jnp.asarray(SELECTION, jnp.bfloat16)
    table = lax.dynamic_index_in_dim(jnp.asarray(SPREAD, jnp.bfloat16), c, keepdims=False)

    weight = lax.all_to_all(jnp.broadcast_to(w_pair[None], (16, 2, 80, FEAT)), ("x", "y"), 0, 0, tiled=True)
    weight = weight.reshape(4, 2, HALF, FEAT)
    mine, theirs = pl.pallas_call(
        attend_kernel,
        out_shape=(bf16(4, TOK, WIDE), bf16(4, TOK, WIDE)),
        in_specs=[SMEM] + [VMEM] * 6,
        out_specs=(VMEM, VMEM),
        scratch_shapes=[pltpu.VMEM((4 * TOK, FEAT + 128), jnp.bfloat16)],
        compiler_params=ROOMY,
        cost_estimate=pl.CostEstimate(flops=60000000000, bytes_accessed=4000000, transcendentals=0),
        name="attend",
    )(code, qa, qb, kv_own, kv_row, kv_far, select)
    got = move(theirs, lambda x, y, h, c, l: (x, y, h, 1 - c, l))
    keep, send = pl.pallas_call(
        merge_cores_kernel,
        out_shape=(bf16(2, TOK, WIDE), bf16(2, TOK, WIDE)),
        in_specs=[VMEM] * 3,
        out_specs=(VMEM, VMEM),
        compiler_params=PARAMS,
        name="merge_cores",
    )(mine, got, table)
    got = move(send, lambda x, y, h, c, l: (x, y, 1 - h, c, l))
    attended = pl.pallas_call(
        merge_last_kernel,
        out_shape=bf16(TOK, FEAT),
        in_specs=[VMEM] * 3,
        out_specs=VMEM,
        compiler_params=PARAMS,
        name="merge_last",
    )(keep, got, table)
    attended = lax.all_gather(attended, "zl", axis=0, axis_index_groups=[[0, 1, 2, 3], [4, 5, 6, 7]])

    def project(away, attended):
        keep, send = pl.pallas_call(
            functools.partial(project_kernel, away),
            out_shape=(jax.ShapeDtypeStruct((TOK, FEAT), jnp.float32), bf16(TOK, FEAT)),
            in_specs=[SMEM] + [VMEM] * 2,
            out_specs=(VMEM, VMEM),
            compiler_params=PARAMS,
            name="project",
        )((zl // 4).reshape(1), attended, weight)
        got = move(send, lambda x, y, h, c, l: (x, y, h, 1 - c, l))
        return keep + got.astype(jnp.float32)

    there = project(True, attended).astype(jnp.bfloat16)
    far = move(there, lambda x, y, h, c, l: (x, y, h, c, l ^ 4))
    attended, unused = lax.optimization_barrier((attended, there))
    here = project(False, attended)

    level_pick = (jnp.arange(LEVELS, dtype=jnp.int32) == levels[0]).astype(jnp.float32)
    gate_row = jnp.sum(level_pick[:, None] * level_gate, axis=0)
    projected = here + far.astype(jnp.float32)
    return (latents.astype(jnp.float32) + gate_row[None, :] * projected).astype(jnp.bfloat16)


def solution(mesh):
    fine = Mesh(mesh.devices.reshape(SIZES), AXES)
    win = ("x", "y", "zh", "c")
    in_specs = (
        P(win, "zl"),
        P(win, "zl"),
        P(win, "zl"),
        P(win, "zl"),
        P(win, "zl"),
        P(None, "zl"),
        P(win),
        P(win, None),
        P(),
    )
    return jax.shard_map(
        on_device, mesh=fine, in_specs=in_specs, out_specs=P(win, "zl"), check_vma=False
    )
```
